32 devices in a mesh: mem: 4 (over y, x), reg: 8 (over z, core).
Axes of the slice: x: 2, y: 2, z: 4, core: 2. Of those that a mesh axis runs over, the one named last changes fastest.
Arguments:
- ensemble: float32 [256, 8192], P('mem', 'reg'), may hold values from -6 to 6
- obs_pert: float32 [256, 8192], P('mem', 'reg'), may hold values from -45 to 45
- innovation: float32 [8192], P('reg'), may hold values from -6 to 6
- block_list: int32 [32, 8], P(('reg', 'mem')), may hold values from 0 to 63, as said below
- loc_weights: float32 [32, 8, 128], P(('reg', 'mem')), may hold values from 0.05 to 1
Outputs:
- analysis: float32 [256, 8192], P('mem', 'reg')
The draws below stay inside these ranges and needn't reach their ends.
Inputs may be any that keep to these rules, and one draw needn't show every extreme that they name: `block_list`: each patch lists 8 different blocks. The regions split the patches and the blocks each into equal runs in order; a patch lists only blocks of its own region and of the regions just before and after it, and always the first and the last block of its own region.
All inputs are finite; a program needn't handle non-finite values.
Results may differ from the reference program's by a relative error of at most 0.0003.
Values sent between devices are 32-bit elements; how exact they have to be, the bound alone decides.
A program may use at most 64 MiB of HBM per device.

```python
import math
import jax
import jax.numpy as jnp
from jax import lax

MEMBERS = 256
PATCH = 256
OBS_BLOCK = 128
BLOCKS_PATCH = 8
NEWTON = 8
BLK_REG = 8
PATCHES = 32
POINTS = 8192
BLOCKS = 64
OBS = 8192


def draw_obs_pert(key, part):
    noise_draw = jnp.clip(jax.random.normal(jax.random.fold_in(key, 11), (MEMBERS, OBS), jnp.float32), -5.0, 5.0)
    log_lower = math.log(0.3)
    log_upper = math.log(3.0)
    member_scale = jnp.exp(jax.random.uniform(jax.random.fold_in(key, 12), (MEMBERS, 1), jnp.float32, log_lower, log_upper))
    obs_scale = jnp.exp(jax.random.uniform(jax.random.fold_in(key, 13), (1, OBS), jnp.float32, log_lower, log_upper))
    return jnp.clip(noise_draw * member_scale * obs_scale, -45.0, 45.0)


def draw_block_list(key, part):
    regions = BLOCKS // BLK_REG
    patch_ids = jnp.arange(PATCHES, dtype=jnp.int32)
    region = patch_ids // (PATCHES // regions)
    candidates = jnp.arange(3 * BLK_REG, dtype=jnp.int32)
    global_ids = (region[:, None] - 1) * BLK_REG + candidates[None, :]
    is_valid = (global_ids >= 0) & (global_ids < BLOCKS)
    raw_score = jax.random.randint(jax.random.fold_in(key, 21), (PATCHES, 3 * BLK_REG), 0, 1 << 20, jnp.int32)
    scores = raw_score * (3 * BLK_REG) + candidates[None, :]
    forced = (candidates == BLK_REG) | (candidates == 2 * BLK_REG - 1)
    scores = jnp.where(forced[None, :], (1 << 30) + candidates[None, :], scores)
    scores = jnp.where(is_valid, scores, -1 - candidates[None, :])
    unused_values, picked = lax.top_k(scores, BLOCKS_PATCH)
    chosen = jnp.take_along_axis(global_ids, picked, axis=1)
    return chosen.astype(jnp.int32)


def steps_of(stream_key, extent, pieces, least, top_value):
    def one(axis_at, parts):
        heights = jax.random.uniform(jax.random.fold_in(jax.random.fold_in(stream_key, 6), axis_at), (parts,), jnp.float32, least / len(pieces), top_value / len(pieces))
        return jnp.repeat(jnp.exp(heights), extent[axis_at] // parts).reshape((-1,) + (1,) * (len(extent) - axis_at - 1))

    factor_of = one(*pieces[0])
    for cut in pieces[1:]:
        factor_of = factor_of * one(*cut)
    return factor_of


def bell_draw(own_key, extent, scale, most, shards=(), kind=jnp.bfloat16):
    values = jax.random.normal(own_key, extent, jnp.float32) * scale
    if len(shards) > 0:
        values = steps_of(own_key, extent, shards, -0.22, 0.18) * values
    return jnp.clip(values, min=-most, max=most).astype(kind)


def setup_inputs(seed: int = 0) -> dict:
    streams_of = jax.random.split(jax.random.key(seed), 6)
    ensemble = bell_draw(streams_of[0], (MEMBERS, POINTS), 1.0, 6.0, ((0, 4), (1, 8)), jnp.float32)
    obs_pert = draw_obs_pert(jax.random.fold_in(streams_of[5], 71), 0)
    innovation = bell_draw(streams_of[2], (OBS,), 1.0, 6.0, ((0, 8),), jnp.float32)
    block_list = draw_block_list(jax.random.fold_in(streams_of[5], 71), 0)
    loc_weights = jnp.clip(0.05 + 0.95 * jax.random.uniform(streams_of[4], (PATCHES, BLOCKS_PATCH, OBS_BLOCK), jnp.float32) ** steps_of(streams_of[4], (PATCHES, BLOCKS_PATCH, OBS_BLOCK), ((0, 32),), -0.2, 0.2), 0.05, 1.0)
    return dict(ensemble=ensemble, obs_pert=obs_pert, innovation=innovation, block_list=block_list, loc_weights=loc_weights)


def batched(first, second, form):
    return jnp.einsum(form, first, second, precision=lax.Precision.HIGHEST, preferred_element_type=jnp.float32)

def analyse(columns, blocks, innov_blocks, weights):
    members = columns.shape[0]
    ens_mean = lax.optimization_barrier(jnp.mean(columns, axis=0))
    anomalies = columns - ens_mean[None]
    weighted = blocks * weights[None]
    gram_matrix = batched(weighted, blocks, 'kpo,jpo->pkj')
    drive = batched(weighted, innov_blocks, 'kpo,po->pk')
    identity = jnp.eye(members, dtype=jnp.float32)
    system = identity[None] + gram_matrix / (members - 1.0)
    trace_sum = jnp.trace(system, axis1=1, axis2=2)
    iterate_y = system / trace_sum[:, None, None]
    iterate_z = jnp.broadcast_to(identity[None], system.shape)
    for repeat in range(NEWTON):
        factor = 1.5 * identity[None] - 0.5 * batched(iterate_z, iterate_y, 'pij,pjk->pik')
        iterate_y, iterate_z = (batched(iterate_y, factor, 'pij,pjk->pik'), batched(factor, iterate_z, 'pij,pjk->pik'))
    root = iterate_z / jnp.sqrt(trace_sum)[:, None, None]
    half_step = batched(root, drive, 'pij,pj->pi')
    mean_weights = batched(root, half_step, 'pij,pj->pi') / (members - 1.0)
    transform = root + mean_weights[:, :, None]
    return ens_mean[None] + batched(transform, anomalies, 'pkj,kps->jps')

def reference(ensemble, obs_pert, innovation, block_list, loc_weights):
    members = ensemble.shape[0]
    blocks_all = obs_pert.reshape(members, BLOCKS, OBS_BLOCK)
    innov_all = innovation.reshape(BLOCKS, OBS_BLOCK)

    def one_patch(index):
        columns = lax.dynamic_slice_in_dim(ensemble, index * PATCH, PATCH, 1).reshape(members, 1, PATCH)
        chosen = lax.dynamic_slice_in_dim(block_list, index, 1, 0)
        blocks = jnp.take(blocks_all, chosen, axis=1).reshape(members, 1, BLOCKS_PATCH * OBS_BLOCK)
        innov_blocks = jnp.take(innov_all, chosen, axis=0).reshape(1, BLOCKS_PATCH * OBS_BLOCK)
        weights = lax.dynamic_slice_in_dim(loc_weights, index, 1, 0).reshape(1, BLOCKS_PATCH * OBS_BLOCK)
        return analyse(columns, blocks, innov_blocks, weights)[:, 0, :]
    result = lax.map(one_patch, jnp.arange(PATCHES, dtype=jnp.int32))
    return jnp.transpose(result, (1, 0, 2)).reshape(members, PATCHES * PATCH)
```

```python
import functools

import jax
import jax.numpy as jnp
from jax import lax
from jax.experimental import pallas as pl
from jax.experimental.pallas import tpu as pltpu
from jax.sharding import PartitionSpec as P

NEWTON = 8
MESH = pl.DeviceIdType.MESH
NN = (((1,), (0,)), ((), ()))
NT = (((1,), (1,)), ((), ()))


def halves(value):
    high = value.astype(jnp.bfloat16)
    low = (value - high.astype(jnp.float32)).astype(jnp.bfloat16)
    return high, low


def product(first, second, dims=NN):
    dot = functools.partial(
        lax.dot_general, dimension_numbers=dims, preferred_element_type=jnp.float32
    )
    return dot(first[0], second[0]) + (dot(first[0], second[1]) + dot(first[1], second[0]))


def flipped(index, mask):
    bit = 1
    while bit <= mask:
        if mask & bit:
            index = index + bit * (1 - 2 * (lax.div(index, bit) % 2))
        bit *= 2
    return index


def kernel(
    n_mem, n_reg, block_ref, ens_ref, obs_ref, innov_ref, weight_ref, out_ref,
    obs_all, innov_all, columns, result, gram, drive_parts,
    local_sem, obs_send, obs_recv, halo_send, halo_recv, innov_send, innov_recv,
    ens_send, ens_recv, out_send, out_recv,
):
    me, region = lax.axis_index("mem"), lax.axis_index("reg")
    rows = obs_ref.shape[0]
    members = n_mem * rows
    own_obs = obs_ref.shape[1]
    points = columns.shape[1]
    listed, width = weight_ref.shape
    own_blocks = own_obs // width
    has_before, has_after = region > 0, region < n_reg - 1
    sides = ((has_before, region - 1, 0), (has_after, region + 1, 1))

    def rows_of(which):
        return pl.ds(pl.multiple_of(which * rows, rows), rows)

    def points_of(which):
        return pl.ds(pl.multiple_of(which * points, points), points)

    barrier = pltpu.get_barrier_semaphore()
    for step in range(1, n_mem):
        pl.semaphore_signal(
            barrier, inc=1, device_id=(flipped(me, step), region), device_id_type=MESH
        )
    for there, other, side in sides:
        @pl.when(there)
        def _():
            pl.semaphore_signal(barrier, inc=1, device_id=(me, other), device_id_type=MESH)

    own_obs_copy = pltpu.make_async_copy(obs_ref, obs_all.at[1, rows_of(me)], local_sem.at[0])
    own_obs_copy.start()
    own_innov_copy = pltpu.make_async_copy(innov_ref, innov_all.at[1], local_sem.at[1])
    own_innov_copy.start()
    own_ens_copy = pltpu.make_async_copy(
        ens_ref.at[:, points_of(me)], columns.at[rows_of(me)], local_sem.at[2]
    )
    own_ens_copy.start()

    near = has_before.astype(jnp.int32) + has_after.astype(jnp.int32)
    pl.semaphore_wait(barrier, n_mem - 1 + near)

    def gather(step):
        return pltpu.make_async_remote_copy(
            src_ref=obs_ref, dst_ref=obs_all.at[1, rows_of(me)],
            send_sem=obs_send.at[step], recv_sem=obs_recv.at[step],
            device_id=(flipped(me, step), region), device_id_type=MESH,
        )

    def halo(step, other, side):
        piece = rows_of(flipped(me, step))
        return pltpu.make_async_remote_copy(
            src_ref=obs_ref if step == 0 else obs_all.at[1, piece],
            dst_ref=obs_all.at[2 - 2 * side, piece],
            send_sem=halo_send.at[side, step], recv_sem=halo_recv.at[side, step],
            device_id=(me, other), device_id_type=MESH,
        )

    def innov(other, side):
        return pltpu.make_async_remote_copy(
            src_ref=innov_ref, dst_ref=innov_all.at[2 - 2 * side],
            send_sem=innov_send.at[side], recv_sem=innov_recv.at[side],
            device_id=(me, other), device_id_type=MESH,
        )

    def exchange(step):
        other = flipped(me, step)
        return pltpu.make_async_remote_copy(
            src_ref=ens_ref.at[:, points_of(other)], dst_ref=columns.at[rows_of(me)],
            send_sem=ens_send.at[step], recv_sem=ens_recv.at[step],
            device_id=(other, region), device_id_type=MESH,
        )

    def give_back(step):
        other = flipped(me, step)
        return pltpu.make_async_remote_copy(
            src_ref=result.at[rows_of(other)], dst_ref=out_ref.at[:, points_of(me)],
            send_sem=out_send.at[step], recv_sem=out_recv.at[step],
            device_id=(other, region), device_id_type=MESH,
        )

    for step in range(1, n_mem):
        gather(step).start()
    for there, other, side in sides:
        @pl.when(there)
        def _():
            halo(0, other, side).start()
            innov(other, side).start()
    for step in range(1, n_mem):
        exchange(step).start()
    for step in range(1, n_mem):
        gather(step).wait_recv()
        for there, other, side in sides:
            @pl.when(there)
            def _():
                halo(step, other, side).start()

    own_ens_copy.wait()
    for step in range(1, n_mem):
        exchange(step).wait_recv()
    ensemble = columns[...]
    mean = jnp.sum(ensemble, axis=0, keepdims=True) / members
    anomalies = ensemble - mean
    anomaly_halves = halves(anomalies)

    def add_region(slot):
        first = (region - 1 + slot) * own_blocks
        parts = []
        for at in range(own_blocks):
            chosen = jnp.where(block_ref[...] == first + at, weight_ref[...], 0.0)
            parts.append(jnp.sum(chosen, axis=0, keepdims=True))
        block = obs_all[slot]
        scaled = block * jnp.concatenate(parts, axis=1)
        gram[...] += product(halves(scaled), halves(block), NT)
        driven = scaled * innov_all[slot]
        total = driven[:, :width]
        for at in range(1, own_blocks):
            total = total + driven[:, at * width : (at + 1) * width]
        drive_parts[...] += total

    gram[...] = jnp.zeros_like(gram)
    drive_parts[...] = jnp.zeros_like(drive_parts)
    own_obs_copy.wait()
    own_innov_copy.wait()
    add_region(1)
    for there, other, side in sides:
        @pl.when(there)
        def _():
            for step in range(n_mem):
                halo(step, other, 1 - side).wait_recv()
            innov(other, 1 - side).wait_recv()
            add_region(2 * side)

    row_at = lax.broadcasted_iota(jnp.int32, (members, members), 0)
    column_at = lax.broadcasted_iota(jnp.int32, (members, members), 1)
    diagonal = row_at == column_at
    identity = jnp.where(diagonal, 1.0, 0.0)
    drive = jnp.sum(drive_parts[...], axis=1, keepdims=True)

    system = identity + gram[...] / (members - 1.0)
    trace = jnp.sum(jnp.where(diagonal, system, 0.0), axis=0, keepdims=True)
    trace = jnp.sum(trace, axis=1, keepdims=True)
    iterate_y = system / trace
    factor = 1.5 * identity - 0.5 * iterate_y
    factor_halves = halves(factor)
    iterate_y = product(halves(iterate_y), factor_halves)
    iterate_z = factor
    z_halves = factor_halves
    for repeat in range(1, NEWTON):
        y_halves = halves(iterate_y)
        factor_halves = halves(1.5 * identity - 0.5 * product(z_halves, y_halves))
        if repeat < NEWTON - 1:
            iterate_y = product(y_halves, factor_halves)
        iterate_z = product(factor_halves, z_halves)
        z_halves = halves(iterate_z)
    root = iterate_z * lax.rsqrt(trace)
    half_step = jnp.sum(root * drive, axis=0, keepdims=True)
    mean_weights = jnp.sum(root * half_step, axis=1, keepdims=True) / (members - 1.0)
    shift = mean + jnp.sum(anomalies * mean_weights, axis=0, keepdims=True)
    result[...] = shift + product(halves(root), anomaly_halves)

    for step in range(1, n_mem):
        give_back(step).start()
    own_out = pltpu.make_async_copy(
        result.at[rows_of(me)], out_ref.at[:, points_of(me)], local_sem.at[3]
    )
    own_out.start()
    for step in range(1, n_mem):
        gather(step).wait_send()
        exchange(step).wait_send()
    for there, other, side in sides:
        @pl.when(there)
        def _():
            for step in range(n_mem):
                halo(step, other, side).wait_send()
            innov(other, side).wait_send()
    own_out.wait()
    for step in range(1, n_mem):
        give_back(step).wait()


def on_device(ensemble, obs_pert, innovation, block_list, loc_weights):
    n_mem, n_reg = lax.axis_size("mem"), lax.axis_size("reg")
    rows, own_points = ensemble.shape
    own_obs = obs_pert.shape[1]
    listed, width = loc_weights.shape[1:]
    members, points = rows * n_mem, own_points // n_mem
    return pl.pallas_call(
        functools.partial(kernel, n_mem, n_reg),
        out_shape=jax.ShapeDtypeStruct((rows, own_points), jnp.float32),
        in_specs=[
            pl.BlockSpec(memory_space=pltpu.VMEM),
            pl.BlockSpec(memory_space=pl.ANY),
            pl.BlockSpec(memory_space=pl.ANY),
            pl.BlockSpec(memory_space=pltpu.VMEM),
            pl.BlockSpec(memory_space=pltpu.VMEM),
        ],
        out_specs=pl.BlockSpec(memory_space=pl.ANY),
        scratch_shapes=[
            pltpu.VMEM((3, members, own_obs), jnp.float32),
            pltpu.VMEM((3, 1, own_obs), jnp.float32),
            pltpu.VMEM((members, points), jnp.float32),
            pltpu.VMEM((members, points), jnp.float32),
            pltpu.VMEM((members, members), jnp.float32),
            pltpu.VMEM((members, width), jnp.float32),
            pltpu.SemaphoreType.DMA((4,)),
            pltpu.SemaphoreType.DMA((n_mem,)),
            pltpu.SemaphoreType.DMA((n_mem,)),
            pltpu.SemaphoreType.DMA((2, n_mem)),
            pltpu.SemaphoreType.DMA((2, n_mem)),
            pltpu.SemaphoreType.DMA((2,)),
            pltpu.SemaphoreType.DMA((2,)),
            pltpu.SemaphoreType.DMA((n_mem,)),
            pltpu.SemaphoreType.DMA((n_mem,)),
            pltpu.SemaphoreType.DMA((n_mem,)),
            pltpu.SemaphoreType.DMA((n_mem,)),
        ],
        compiler_params=pltpu.CompilerParams(
            collective_id=0, has_side_effects=True, vmem_limit_bytes=32 * 2**20
        ),
    )(
        block_list.reshape(listed, 1), ensemble, obs_pert,
        innovation.reshape(1, own_obs), loc_weights.reshape(listed, width),
    )


def solution(mesh):
    return jax.shard_map(
        on_device,
        mesh=mesh,
        in_specs=(
            P("mem", "reg"),
            P("mem", "reg"),
            P("reg"),
            P(("reg", "mem"), None),
            P(("reg", "mem"), None, None),
        ),
        out_specs=P("mem", "reg"),
        check_vma=False,
    )
```

```python
import functools

import jax
import jax.numpy as jnp
from jax import lax
from jax.experimental import pallas as pl
from jax.experimental.pallas import tpu as pltpu
from jax.sharding import PartitionSpec as P

NEWTON = 8
MESH = pl.DeviceIdType.MESH
NN = (((1,), (0,)), ((), ()))
NT = (((1,), (1,)), ((), ()))


def halves(value):
    high = value.astype(jnp.bfloat16)
    low = (value - high.astype(jnp.float32)).astype(jnp.bfloat16)
    return high, low


def product(first, second, dims=NN):
    dot = functools.partial(
        lax.dot_general, dimension_numbers=dims, preferred_element_type=jnp.float32
    )
    return dot(first[0], second[0]) + (dot(first[0], second[1]) + dot(first[1], second[0]))


def flipped(index, mask):
    bit = 1
    while bit <= mask:
        if mask & bit:
            index = index + bit * (1 - 2 * (lax.div(index, bit) % 2))
        bit *= 2
    return index


def kernel(
    n_mem, n_reg, block_ref, ens_ref, obs_ref, innov_ref, weight_ref, out_ref,
    obs_all, innov_all, columns, result, gram, drive_parts,
    local_sem, obs_send, obs_recv, halo_send, halo_recv, innov_send, innov_recv,
    ens_send, ens_recv, out_send, out_recv,
):
    me, region = lax.axis_index("mem"), lax.axis_index("reg")
    rows = obs_ref.shape[0]
    members = n_mem * rows
    own_obs = obs_ref.shape[1]
    points = columns.shape[1]
    listed, width = weight_ref.shape
    own_blocks = own_obs // width
    has_before, has_after = region > 0, region < n_reg - 1
    sides = ((has_before, region - 1, 0), (has_after, region + 1, 1))

    def rows_of(which):
        return pl.ds(pl.multiple_of(which * rows, rows), rows)

    def points_of(which):
        return pl.ds(pl.multiple_of(which * points, points), points)

    barrier = pltpu.get_barrier_semaphore()
    for step in range(1, n_mem):
        pl.semaphore_signal(
            barrier, inc=1, device_id=(flipped(me, step), region), device_id_type=MESH
        )
    for there, other, side in sides:
        @pl.when(there)
        def _():
            pl.semaphore_signal(barrier, inc=1, device_id=(me, other), device_id_type=MESH)

    own_obs_copy = pltpu.make_async_copy(obs_ref, obs_all.at[1, rows_of(me)], local_sem.at[0])
    own_obs_copy.start()
    own_innov_copy = pltpu.make_async_copy(innov_ref, innov_all.at[1], local_sem.at[1])
    own_innov_copy.start()
    own_ens_copy = pltpu.make_async_copy(
        ens_ref.at[:, points_of(me)], columns.at[rows_of(me)], local_sem.at[2]
    )
    own_ens_copy.start()

    near = has_before.astype(jnp.int32) + has_after.astype(jnp.int32)
    pl.semaphore_wait(barrier, n_mem - 1 + near)

    def gather(step):
        return pltpu.make_async_remote_copy(
            src_ref=obs_ref, dst_ref=obs_all.at[1, rows_of(me)],
            send_sem=obs_send.at[step], recv_sem=obs_recv.at[step],
            device_id=(flipped(me, step), region), device_id_type=MESH,
        )

    def halo(step, other, side):
        piece = rows_of(flipped(me, step))
        return pltpu.make_async_remote_copy(
            src_ref=obs_ref if step == 0 else obs_all.at[1, piece],
            dst_ref=obs_all.at[2 - 2 * side, piece],
            send_sem=halo_send.at[side, step], recv_sem=halo_recv.at[side, step],
            device_id=(me, other), device_id_type=MESH,
        )

    def innov(other, side):
        return pltpu.make_async_remote_copy(
            src_ref=innov_ref, dst_ref=innov_all.at[2 - 2 * side],
            send_sem=innov_send.at[side], recv_sem=innov_recv.at[side],
            device_id=(me, other), device_id_type=MESH,
        )

    def exchange(step):
        other = flipped(me, step)
        return pltpu.make_async_remote_copy(
            src_ref=ens_ref.at[:, points_of(other)], dst_ref=columns.at[rows_of(me)],
            send_sem=ens_send.at[step], recv_sem=ens_recv.at[step],
            device_id=(other, region), device_id_type=MESH,
        )

    def give_back(step):
        other = flipped(me, step)
        return pltpu.make_async_remote_copy(
            src_ref=result.at[rows_of(other)], dst_ref=out_ref.at[:, points_of(me)],
            send_sem=out_send.at[step], recv_sem=out_recv.at[step],
            device_id=(other, region), device_id_type=MESH,
        )

    for step in range(1, n_mem):
        gather(step).start()
    for there, other, side in sides:
        @pl.when(there)
        def _():
            halo(0, other, side).start()
            innov(other, side).start()
    for step in range(1, n_mem):
        exchange(step).start()
    for step in range(1, n_mem):
        gather(step).wait_recv()
        for there, other, side in sides:
            @pl.when(there)
            def _():
                halo(step, other, side).start()

    own_ens_copy.wait()
    for step in range(1, n_mem):
        exchange(step).wait_recv()
    ensemble = columns[...]
    mean = jnp.sum(ensemble, axis=0, keepdims=True) / members
    anomalies = ensemble - mean
    anomaly_halves = halves(anomalies)

    def add_region(slot):
        first = (region - 1 + slot) * own_blocks
        parts = []
        for at in range(own_blocks):
            chosen = jnp.where(block_ref[...] == first + at, weight_ref[...], 0.0)
            parts.append(jnp.sum(chosen, axis=0, keepdims=True))
        block = obs_all[slot]
        scaled = block * jnp.concatenate(parts, axis=1)
        gram[...] += product(halves(scaled), halves(block), NT)
        driven = scaled * innov_all[slot]
        total = driven[:, :width]
        for at in range(1, own_blocks):
            total = total + driven[:, at * width : (at + 1) * width]
        drive_parts[...] += total

    gram[...] = jnp.zeros_like(gram)
    drive_parts[...] = jnp.zeros_like(drive_parts)
    own_obs_copy.wait()
    own_innov_copy.wait()
    add_region(1)
    for there, other, side in sides:
        @pl.when(there)
        def _():
            for step in range(n_mem):
                halo(step, other, 1 - side).wait_recv()
            innov(other, 1 - side).wait_recv()
            add_region(2 * side)

    row_at = lax.broadcasted_iota(jnp.int32, (members, members), 0)
    column_at = lax.broadcasted_iota(jnp.int32, (members, members), 1)
    diagonal = row_at == column_at
    identity = jnp.where(diagonal, 1.0, 0.0)
    drive = jnp.sum(drive_parts[...], axis=1, keepdims=True)

    system = identity + gram[...] / (members - 1.0)
    trace = jnp.sum(jnp.where(diagonal, system, 0.0), axis=0, keepdims=True)
    trace = jnp.sum(trace, axis=1, keepdims=True)
    iterate_y = system / trace
    factor = 1.5 * identity - 0.5 * iterate_y
    factor_halves = halves(factor)
    iterate_y = product(halves(iterate_y), factor_halves)
    iterate_z = factor
    z_halves = factor_halves
    for repeat in range(1, NEWTON):
        y_halves = halves(iterate_y)
        factor_halves = halves(1.5 * identity - 0.5 * product(z_halves, y_halves))
        if repeat < NEWTON - 1:
            iterate_y = product(y_halves, factor_halves)
        iterate_z = product(factor_halves, z_halves)
        z_halves = halves(iterate_z)
    root = iterate_z * lax.rsqrt(trace)
    half_step = jnp.sum(root * drive, axis=0, keepdims=True)
    mean_weights = jnp.sum(root * half_step, axis=1, keepdims=True) / (members - 1.0)
    shift = mean + jnp.sum(anomalies * mean_weights, axis=0, keepdims=True)
    result[...] = shift + product(halves(root), anomaly_halves)

    for step in range(1, n_mem):
        give_back(step).start()
    own_out = pltpu.make_async_copy(
        result.at[rows_of(me)], out_ref.at[:, points_of(me)], local_sem.at[3]
    )
    own_out.start()
    for step in range(1, n_mem):
        gather(step).wait_send()
        exchange(step).wait_send()
    for there, other, side in sides:
        @pl.when(there)
        def _():
            for step in range(n_mem):
                halo(step, other, side).wait_send()
            innov(other, side).wait_send()
    own_out.wait()
    for step in range(1, n_mem):
        give_back(step).wait()


def on_device(ensemble, obs_pert, innovation, block_list, loc_weights):
    n_mem, n_reg = lax.axis_size("mem"), lax.axis_size("reg")
    rows, own_points = ensemble.shape
    own_obs = obs_pert.shape[1]
    listed, width = loc_weights.shape[1:]
    members, points = rows * n_mem, own_points // n_mem
    return pl.pallas_call(
        functools.partial(kernel, n_mem, n_reg),
        out_shape=jax.ShapeDtypeStruct((rows, own_points), jnp.float32),
        in_specs=[
            pl.BlockSpec(memory_space=pltpu.VMEM),
            pl.BlockSpec(memory_space=pl.ANY),
            pl.BlockSpec(memory_space=pl.ANY),
            pl.BlockSpec(memory_space=pltpu.VMEM),
            pl.BlockSpec(memory_space=pltpu.VMEM),
        ],
        out_specs=pl.BlockSpec(memory_space=pl.ANY),
        scratch_shapes=[
            pltpu.VMEM((3, members, own_obs), jnp.float32),
            pltpu.VMEM((3, 1, own_obs), jnp.float32),
            pltpu.VMEM((members, points), jnp.float32),
            pltpu.VMEM((members, points), jnp.float32),
            pltpu.VMEM((members, members), jnp.float32),
            pltpu.VMEM((members, width), jnp.float32),
            pltpu.SemaphoreType.DMA((4,)),
            pltpu.SemaphoreType.DMA((n_mem,)),
            pltpu.SemaphoreType.DMA((n_mem,)),
            pltpu.SemaphoreType.DMA((2, n_mem)),
            pltpu.SemaphoreType.DMA((2, n_mem)),
            pltpu.SemaphoreType.DMA((2,)),
            pltpu.SemaphoreType.DMA((2,)),
            pltpu.SemaphoreType.DMA((n_mem,)),
            pltpu.SemaphoreType.DMA((n_mem,)),
            pltpu.SemaphoreType.DMA((n_mem,)),
            pltpu.SemaphoreType.DMA((n_mem,)),
        ],
        compiler_params=pltpu.CompilerParams(
            collective_id=0, has_side_effects=True, vmem_limit_bytes=60 * 2**20
        ),
    )(
        block_list.reshape(listed, 1), ensemble, obs_pert,
        innovation.reshape(1, own_obs), loc_weights.reshape(listed, width),
    )


def solution(mesh):
    return jax.shard_map(
        on_device,
        mesh=mesh,
        in_specs=(
            P("mem", "reg"),
            P("mem", "reg"),
            P("reg"),
            P(("reg", "mem"), None),
            P(("reg", "mem"), None, None),
        ),
        out_specs=P("mem", "reg"),
        check_vma=False,
    )
```

```python
import functools

import jax
import jax.numpy as jnp
from jax import lax
from jax.experimental import pallas as pl
from jax.experimental.pallas import tpu as pltpu
from jax.sharding import PartitionSpec as P

NEWTON = 8
MESH = pl.DeviceIdType.MESH
NN = (((1,), (0,)), ((), ()))
NT = (((1,), (1,)), ((), ()))


def halves(value):
    high = value.astype(jnp.bfloat16)
    low = (value - high.astype(jnp.float32)).astype(jnp.bfloat16)
    return high, low


def product(first, second, dims=NN):
    dot = functools.partial(
        lax.dot_general, dimension_numbers=dims, preferred_element_type=jnp.float32
    )
    return dot(first[0], second[0]) + (dot(first[0], second[1]) + dot(first[1], second[0]))


def flipped(index, mask):
    bit = 1
    while bit <= mask:
        if mask & bit:
            index = index + bit * (1 - 2 * (lax.div(index, bit) % 2))
        bit *= 2
    return index


def kernel(
    n_mem, n_reg, block_ref, ens_ref, obs_ref, innov_ref, weight_ref, out_ref,
    obs_all, innov_all, columns, result, gram, drive_parts,
    local_sem, obs_send, obs_recv, halo_send, halo_recv, innov_send, innov_recv,
    ens_send, ens_recv, out_send, out_recv,
):
    me, region = lax.axis_index("mem"), lax.axis_index("reg")
    rows = obs_ref.shape[0]
    members = n_mem * rows
    own_obs = obs_ref.shape[1]
    points = columns.shape[1]
    listed, width = weight_ref.shape
    own_blocks = own_obs // width
    has_before, has_after = region > 0, region < n_reg - 1
    sides = ((has_before, region - 1, 0), (has_after, region + 1, 1))

    def rows_of(which):
        return pl.ds(pl.multiple_of(which * rows, rows), rows)

    parts_in = obs_send.shape[1]
    part = rows // parts_in

    def part_of(which, at):
        return pl.ds(pl.multiple_of(which * rows + at * part, part), part)

    def points_of(which):
        return pl.ds(pl.multiple_of(which * points, points), points)

    barrier = pltpu.get_barrier_semaphore()
    for step in range(1, n_mem):
        pl.semaphore_signal(
            barrier, inc=1, device_id=(flipped(me, step), region), device_id_type=MESH
        )
    for there, other, side in sides:
        @pl.when(there)
        def _():
            pl.semaphore_signal(barrier, inc=1, device_id=(me, other), device_id_type=MESH)

    own_obs_copy = pltpu.make_async_copy(obs_ref, obs_all.at[1, rows_of(me)], local_sem.at[0])
    own_obs_copy.start()
    own_innov_copy = pltpu.make_async_copy(innov_ref, innov_all.at[1], local_sem.at[1])
    own_innov_copy.start()
    own_ens_copy = pltpu.make_async_copy(
        ens_ref.at[:, points_of(me)], columns.at[rows_of(me)], local_sem.at[2]
    )
    own_ens_copy.start()

    near = has_before.astype(jnp.int32) + has_after.astype(jnp.int32)
    pl.semaphore_wait(barrier, n_mem - 1 + near)

    def gather(step, at):
        return pltpu.make_async_remote_copy(
            src_ref=obs_ref.at[pl.ds(at * part, part)], dst_ref=obs_all.at[1, part_of(me, at)],
            send_sem=obs_send.at[step, at], recv_sem=obs_recv.at[step, at],
            device_id=(flipped(me, step), region), device_id_type=MESH,
        )

    def halo(step, at, other, side):
        piece = part_of(flipped(me, step), at)
        return pltpu.make_async_remote_copy(
            src_ref=obs_ref.at[pl.ds(at * part, part)] if step == 0 else obs_all.at[1, piece],
            dst_ref=obs_all.at[2 - 2 * side, piece],
            send_sem=halo_send.at[side, step, at], recv_sem=halo_recv.at[side, step, at],
            device_id=(me, other), device_id_type=MESH,
        )

    def innov(other, side):
        return pltpu.make_async_remote_copy(
            src_ref=innov_ref, dst_ref=innov_all.at[2 - 2 * side],
            send_sem=innov_send.at[side], recv_sem=innov_recv.at[side],
            device_id=(me, other), device_id_type=MESH,
        )

    def exchange(step):
        other = flipped(me, step)
        return pltpu.make_async_remote_copy(
            src_ref=ens_ref.at[:, points_of(other)], dst_ref=columns.at[rows_of(me)],
            send_sem=ens_send.at[step], recv_sem=ens_recv.at[step],
            device_id=(other, region), device_id_type=MESH,
        )

    def give_back(step):
        other = flipped(me, step)
        return pltpu.make_async_remote_copy(
            src_ref=result.at[rows_of(other)], dst_ref=out_ref.at[:, points_of(me)],
            send_sem=out_send.at[step], recv_sem=out_recv.at[step],
            device_id=(other, region), device_id_type=MESH,
        )

    for at in range(parts_in):
        for step in range(1, n_mem):
            gather(step, at).start()
    for there, other, side in sides:
        @pl.when(there)
        def _():
            for at in range(parts_in):
                halo(0, at, other, side).start()
            innov(other, side).start()
    for step in range(1, n_mem):
        exchange(step).start()
    for at in range(parts_in):
        for step in range(1, n_mem):
            gather(step, at).wait_recv()
            for there, other, side in sides:
                @pl.when(there)
                def _():
                    halo(step, at, other, side).start()

    own_ens_copy.wait()
    for step in range(1, n_mem):
        exchange(step).wait_recv()
    ensemble = columns[...]
    mean = jnp.sum(ensemble, axis=0, keepdims=True) / members
    anomalies = ensemble - mean
    anomaly_halves = halves(anomalies)

    def add_region(slot):
        first = (region - 1 + slot) * own_blocks
        parts = []
        for at in range(own_blocks):
            chosen = jnp.where(block_ref[...] == first + at, weight_ref[...], 0.0)
            parts.append(jnp.sum(chosen, axis=0, keepdims=True))
        block = obs_all[slot]
        scaled = block * jnp.concatenate(parts, axis=1)
        gram[...] += product(halves(scaled), halves(block), NT)
        driven = scaled * innov_all[slot]
        total = driven[:, :width]
        for at in range(1, own_blocks):
            total = total + driven[:, at * width : (at + 1) * width]
        drive_parts[...] += total

    gram[...] = jnp.zeros_like(gram)
    drive_parts[...] = jnp.zeros_like(drive_parts)
    own_obs_copy.wait()
    own_innov_copy.wait()
    add_region(1)
    for there, other, side in sides:
        @pl.when(there)
        def _():
            for step in range(n_mem):
                for at in range(parts_in):
                    halo(step, at, other, 1 - side).wait_recv()
            innov(other, 1 - side).wait_recv()
            add_region(2 * side)

    row_at = lax.broadcasted_iota(jnp.int32, (members, members), 0)
    column_at = lax.broadcasted_iota(jnp.int32, (members, members), 1)
    diagonal = row_at == column_at
    identity = jnp.where(diagonal, 1.0, 0.0)
    drive = jnp.sum(drive_parts[...], axis=1, keepdims=True)

    system = identity + gram[...] / (members - 1.0)
    trace = jnp.sum(jnp.where(diagonal, system, 0.0), axis=0, keepdims=True)
    trace = jnp.sum(trace, axis=1, keepdims=True)
    iterate_y = system / trace
    factor = 1.5 * identity - 0.5 * iterate_y
    factor_halves = halves(factor)
    iterate_y = product(halves(iterate_y), factor_halves)
    iterate_z = factor
    z_halves = factor_halves
    for repeat in range(1, NEWTON):
        y_halves = halves(iterate_y)
        factor_halves = halves(1.5 * identity - 0.5 * product(z_halves, y_halves))
        if repeat < NEWTON - 1:
            iterate_y = product(y_halves, factor_halves)
        iterate_z = product(factor_halves, z_halves)
        z_halves = halves(iterate_z)
    root = iterate_z * lax.rsqrt(trace)
    half_step = jnp.sum(root * drive, axis=0, keepdims=True)
    mean_weights = jnp.sum(root * half_step, axis=1, keepdims=True) / (members - 1.0)
    shift = mean + jnp.sum(anomalies * mean_weights, axis=0, keepdims=True)
    result[...] = shift + product(halves(root), anomaly_halves)

    for step in range(1, n_mem):
        give_back(step).start()
    own_out = pltpu.make_async_copy(
        result.at[rows_of(me)], out_ref.at[:, points_of(me)], local_sem.at[3]
    )
    own_out.start()
    for step in range(1, n_mem):
        for at in range(parts_in):
            gather(step, at).wait_send()
        exchange(step).wait_send()
    for there, other, side in sides:
        @pl.when(there)
        def _():
            for step in range(n_mem):
                for at in range(parts_in):
                    halo(step, at, other, side).wait_send()
            innov(other, side).wait_send()
    own_out.wait()
    for step in range(1, n_mem):
        give_back(step).wait()


def on_device(ensemble, obs_pert, innovation, block_list, loc_weights):
    n_mem, n_reg = lax.axis_size("mem"), lax.axis_size("reg")
    rows, own_points = ensemble.shape
    own_obs = obs_pert.shape[1]
    listed, width = loc_weights.shape[1:]
    members, points = rows * n_mem, own_points // n_mem
    parts_in = 2 if rows % 16 == 0 else 1
    return pl.pallas_call(
        functools.partial(kernel, n_mem, n_reg),
        out_shape=jax.ShapeDtypeStruct((rows, own_points), jnp.float32),
        in_specs=[
            pl.BlockSpec(memory_space=pltpu.VMEM),
            pl.BlockSpec(memory_space=pl.ANY),
            pl.BlockSpec(memory_space=pl.ANY),
            pl.BlockSpec(memory_space=pltpu.VMEM),
            pl.BlockSpec(memory_space=pltpu.VMEM),
        ],
        out_specs=pl.BlockSpec(memory_space=pl.ANY),
        scratch_shapes=[
            pltpu.VMEM((3, members, own_obs), jnp.float32),
            pltpu.VMEM((3, 1, own_obs), jnp.float32),
            pltpu.VMEM((members, points), jnp.float32),
            pltpu.VMEM((members, points), jnp.float32),
            pltpu.VMEM((members, members), jnp.float32),
            pltpu.VMEM((members, width), jnp.float32),
            pltpu.SemaphoreType.DMA((4,)),
            pltpu.SemaphoreType.DMA((n_mem, parts_in)),
            pltpu.SemaphoreType.DMA((n_mem, parts_in)),
            pltpu.SemaphoreType.DMA((2, n_mem, parts_in)),
            pltpu.SemaphoreType.DMA((2, n_mem, parts_in)),
            pltpu.SemaphoreType.DMA((2,)),
            pltpu.SemaphoreType.DMA((2,)),
            pltpu.SemaphoreType.DMA((n_mem,)),
            pltpu.SemaphoreType.DMA((n_mem,)),
            pltpu.SemaphoreType.DMA((n_mem,)),
            pltpu.SemaphoreType.DMA((n_mem,)),
        ],
        compiler_params=pltpu.CompilerParams(
            collective_id=0, has_side_effects=True, vmem_limit_bytes=32 * 2**20
        ),
    )(
        block_list.reshape(listed, 1), ensemble, obs_pert,
        innovation.reshape(1, own_obs), loc_weights.reshape(listed, width),
    )


def solution(mesh):
    return jax.shard_map(
        on_device,
        mesh=mesh,
        in_specs=(
            P("mem", "reg"),
            P("mem", "reg"),
            P("reg"),
            P(("reg", "mem"), None),
            P(("reg", "mem"), None, None),
        ),
        out_specs=P("mem", "reg"),
        check_vma=False,
    )
```

```python
import functools

import jax
import jax.numpy as jnp
from jax import lax
from jax.experimental import pallas as pl
from jax.experimental.pallas import tpu as pltpu
from jax.sharding import PartitionSpec as P

NEWTON = 8
MESH = pl.DeviceIdType.MESH
NN = (((1,), (0,)), ((), ()))
NT = (((1,), (1,)), ((), ()))


def halves(value):
    high = value.astype(jnp.bfloat16)
    low = (value - high.astype(jnp.float32)).astype(jnp.bfloat16)
    return high, low


def product(first, second, dims=NN):
    dot = functools.partial(
        lax.dot_general, dimension_numbers=dims, preferred_element_type=jnp.float32
    )
    return dot(first[0], second[0]) + (dot(first[0], second[1]) + dot(first[1], second[0]))


def stacked(firsts, second):
    dot = functools.partial(jnp.dot, preferred_element_type=jnp.float32)
    size, count = second[0].shape[0], len(firsts)
    highs = [first[0] for first in firsts]
    wide = dot(jnp.concatenate(highs + [first[1] for first in firsts], axis=0), second[0])
    thin = dot(jnp.concatenate(highs, axis=0) if count > 1 else highs[0], second[1])
    return [
        wide[at * size : (at + 1) * size]
        + (thin[at * size : (at + 1) * size] + wide[(count + at) * size : (count + at + 1) * size])
        for at in range(count)
    ]


def flipped(index, mask):
    bit = 1
    while bit <= mask:
        if mask & bit:
            index = index + bit * (1 - 2 * (lax.div(index, bit) % 2))
        bit *= 2
    return index


def kernel(
    n_mem, n_reg, block_ref, ens_ref, obs_ref, innov_ref, weight_ref, out_ref,
    obs_all, innov_all, columns, result, gram, drive_parts,
    local_sem, obs_send, obs_recv, halo_send, halo_recv, innov_send, innov_recv,
    ens_send, ens_recv, out_send, out_recv,
):
    me, region = lax.axis_index("mem"), lax.axis_index("reg")
    rows = obs_ref.shape[0]
    members = n_mem * rows
    own_obs = obs_ref.shape[1]
    points = columns.shape[1]
    listed, width = weight_ref.shape
    own_blocks = own_obs // width
    has_before, has_after = region > 0, region < n_reg - 1
    sides = ((has_before, region - 1, 0), (has_after, region + 1, 1))

    def rows_of(which):
        return pl.ds(pl.multiple_of(which * rows, rows), rows)

    parts_in = obs_send.shape[1]
    part = rows // parts_in

    def part_of(which, at):
        return pl.ds(pl.multiple_of(which * rows + at * part, part), part)

    def points_of(which):
        return pl.ds(pl.multiple_of(which * points, points), points)

    barrier = pltpu.get_barrier_semaphore()
    for step in range(1, n_mem):
        pl.semaphore_signal(
            barrier, inc=1, device_id=(flipped(me, step), region), device_id_type=MESH
        )
    for there, other, side in sides:
        @pl.when(there)
        def _():
            pl.semaphore_signal(barrier, inc=1, device_id=(me, other), device_id_type=MESH)

    own_obs_copy = pltpu.make_async_copy(obs_ref, obs_all.at[1, rows_of(me)], local_sem.at[0])
    own_obs_copy.start()
    own_innov_copy = pltpu.make_async_copy(innov_ref, innov_all.at[1], local_sem.at[1])
    own_innov_copy.start()
    own_ens_copy = pltpu.make_async_copy(
        ens_ref.at[:, points_of(me)], columns.at[rows_of(me)], local_sem.at[2]
    )
    own_ens_copy.start()

    near = has_before.astype(jnp.int32) + has_after.astype(jnp.int32)
    pl.semaphore_wait(barrier, n_mem - 1 + near)

    def gather(step, at):
        return pltpu.make_async_remote_copy(
            src_ref=obs_ref.at[pl.ds(at * part, part)], dst_ref=obs_all.at[1, part_of(me, at)],
            send_sem=obs_send.at[step, at], recv_sem=obs_recv.at[step, at],
            device_id=(flipped(me, step), region), device_id_type=MESH,
        )

    def halo(step, at, other, side):
        piece = part_of(flipped(me, step), at)
        return pltpu.make_async_remote_copy(
            src_ref=obs_ref.at[pl.ds(at * part, part)] if step == 0 else obs_all.at[1, piece],
            dst_ref=obs_all.at[2 - 2 * side, piece],
            send_sem=halo_send.at[side, step, at], recv_sem=halo_recv.at[side, step, at],
            device_id=(me, other), device_id_type=MESH,
        )

    def innov(other, side):
        return pltpu.make_async_remote_copy(
            src_ref=innov_ref, dst_ref=innov_all.at[2 - 2 * side],
            send_sem=innov_send.at[side], recv_sem=innov_recv.at[side],
            device_id=(me, other), device_id_type=MESH,
        )

    def exchange(step):
        other = flipped(me, step)
        return pltpu.make_async_remote_copy(
            src_ref=ens_ref.at[:, points_of(other)], dst_ref=columns.at[rows_of(me)],
            send_sem=ens_send.at[step], recv_sem=ens_recv.at[step],
            device_id=(other, region), device_id_type=MESH,
        )

    def give_back(step):
        other = flipped(me, step)
        return pltpu.make_async_remote_copy(
            src_ref=result.at[rows_of(other)], dst_ref=out_ref.at[:, points_of(me)],
            send_sem=out_send.at[step], recv_sem=out_recv.at[step],
            device_id=(other, region), device_id_type=MESH,
        )

    for at in range(parts_in):
        for step in range(1, n_mem):
            gather(step, at).start()
    for there, other, side in sides:
        @pl.when(there)
        def _():
            for at in range(parts_in):
                halo(0, at, other, side).start()
            innov(other, side).start()
    for step in range(1, n_mem):
        exchange(step).start()
    for at in range(parts_in):
        for step in range(1, n_mem):
            gather(step, at).wait_recv()
            for there, other, side in sides:
                @pl.when(there)
                def _():
                    halo(step, at, other, side).start()

    own_ens_copy.wait()
    for step in range(1, n_mem):
        exchange(step).wait_recv()
    ensemble = columns[...]
    mean = jnp.sum(ensemble, axis=0, keepdims=True) / members
    anomalies = ensemble - mean
    anomaly_halves = halves(anomalies)

    def add_region(slot):
        first = (region - 1 + slot) * own_blocks
        parts = []
        for at in range(own_blocks):
            chosen = jnp.where(block_ref[...] == first + at, weight_ref[...], 0.0)
            parts.append(jnp.sum(chosen, axis=0, keepdims=True))
        block = obs_all[slot]
        scaled = block * jnp.concatenate(parts, axis=1)
        gram[...] += product(halves(scaled), halves(block), NT)
        driven = scaled * innov_all[slot]
        total = driven[:, :width]
        for at in range(1, own_blocks):
            total = total + driven[:, at * width : (at + 1) * width]
        drive_parts[...] += total

    gram[...] = jnp.zeros_like(gram)
    drive_parts[...] = jnp.zeros_like(drive_parts)
    own_obs_copy.wait()
    own_innov_copy.wait()
    add_region(1)
    for there, other, side in sides:
        @pl.when(there)
        def _():
            for step in range(n_mem):
                for at in range(parts_in):
                    halo(step, at, other, 1 - side).wait_recv()
            innov(other, 1 - side).wait_recv()
            add_region(2 * side)

    row_at = lax.broadcasted_iota(jnp.int32, (members, members), 0)
    column_at = lax.broadcasted_iota(jnp.int32, (members, members), 1)
    diagonal = row_at == column_at
    identity = jnp.where(diagonal, 1.0, 0.0)
    drive = jnp.sum(drive_parts[...], axis=1, keepdims=True)

    system = identity + gram[...] / (members - 1.0)
    trace = jnp.sum(jnp.where(diagonal, system, 0.0), axis=0, keepdims=True)
    trace = jnp.sum(trace, axis=1, keepdims=True)
    iterate_y = system / trace
    factor = 1.5 * identity - 0.5 * iterate_y
    factor_halves = halves(factor)
    [iterate_y] = stacked([halves(iterate_y)], factor_halves)
    iterate_z = factor
    z_halves = factor_halves
    for repeat in range(1, NEWTON):
        y_halves = halves(iterate_y)
        [both] = stacked([z_halves], y_halves)
        factor_halves = halves(1.5 * identity - 0.5 * both)
        if repeat < NEWTON - 1:
            iterate_y, iterate_z = stacked([y_halves, z_halves], factor_halves)
            z_halves = halves(iterate_z)
        else:
            [iterate_z] = stacked([z_halves], factor_halves)
    root = iterate_z * lax.rsqrt(trace)
    half_step = jnp.sum(root * drive, axis=0, keepdims=True)
    mean_weights = jnp.sum(root * half_step, axis=1, keepdims=True) / (members - 1.0)
    shift = mean + jnp.sum(anomalies * mean_weights, axis=0, keepdims=True)
    result[...] = shift + product(halves(root), anomaly_halves)

    for step in range(1, n_mem):
        give_back(step).start()
    own_out = pltpu.make_async_copy(
        result.at[rows_of(me)], out_ref.at[:, points_of(me)], local_sem.at[3]
    )
    own_out.start()
    for step in range(1, n_mem):
        for at in range(parts_in):
            gather(step, at).wait_send()
        exchange(step).wait_send()
    for there, other, side in sides:
        @pl.when(there)
        def _():
            for step in range(n_mem):
                for at in range(parts_in):
                    halo(step, at, other, side).wait_send()
            innov(other, side).wait_send()
    own_out.wait()
    for step in range(1, n_mem):
        give_back(step).wait()


def on_device(ensemble, obs_pert, innovation, block_list, loc_weights):
    n_mem, n_reg = lax.axis_size("mem"), lax.axis_size("reg")
    rows, own_points = ensemble.shape
    own_obs = obs_pert.shape[1]
    listed, width = loc_weights.shape[1:]
    members, points = rows * n_mem, own_points // n_mem
    parts_in = 2 if rows % 16 == 0 else 1
    return pl.pallas_call(
        functools.partial(kernel, n_mem, n_reg),
        out_shape=jax.ShapeDtypeStruct((rows, own_points), jnp.float32),
        in_specs=[
            pl.BlockSpec(memory_space=pltpu.VMEM),
            pl.BlockSpec(memory_space=pl.ANY),
            pl.BlockSpec(memory_space=pl.ANY),
            pl.BlockSpec(memory_space=pltpu.VMEM),
            pl.BlockSpec(memory_space=pltpu.VMEM),
        ],
        out_specs=pl.BlockSpec(memory_space=pl.ANY),
        scratch_shapes=[
            pltpu.VMEM((3, members, own_obs), jnp.float32),
            pltpu.VMEM((3, 1, own_obs), jnp.float32),
            pltpu.VMEM((members, points), jnp.float32),
            pltpu.VMEM((members, points), jnp.float32),
            pltpu.VMEM((members, members), jnp.float32),
            pltpu.VMEM((members, width), jnp.float32),
            pltpu.SemaphoreType.DMA((4,)),
            pltpu.SemaphoreType.DMA((n_mem, parts_in)),
            pltpu.SemaphoreType.DMA((n_mem, parts_in)),
            pltpu.SemaphoreType.DMA((2, n_mem, parts_in)),
            pltpu.SemaphoreType.DMA((2, n_mem, parts_in)),
            pltpu.SemaphoreType.DMA((2,)),
            pltpu.SemaphoreType.DMA((2,)),
            pltpu.SemaphoreType.DMA((n_mem,)),
            pltpu.SemaphoreType.DMA((n_mem,)),
            pltpu.SemaphoreType.DMA((n_mem,)),
            pltpu.SemaphoreType.DMA((n_mem,)),
        ],
        compiler_params=pltpu.CompilerParams(
            collective_id=0, has_side_effects=True, vmem_limit_bytes=32 * 2**20
        ),
    )(
        block_list.reshape(listed, 1), ensemble, obs_pert,
        innovation.reshape(1, own_obs), loc_weights.reshape(listed, width),
    )


def solution(mesh):
    return jax.shard_map(
        on_device,
        mesh=mesh,
        in_specs=(
            P("mem", "reg"),
            P("mem", "reg"),
            P("reg"),
            P(("reg", "mem"), None),
            P(("reg", "mem"), None, None),
        ),
        out_specs=P("mem", "reg"),
        check_vma=False,
    )
```

```python
import functools

import jax
import jax.numpy as jnp
from jax import lax
from jax.experimental import pallas as pl
from jax.experimental.pallas import tpu as pltpu
from jax.sharding import PartitionSpec as P

NEWTON = 8
MESH = pl.DeviceIdType.MESH
NN = (((1,), (0,)), ((), ()))
NT = (((1,), (1,)), ((), ()))


def halves(value):
    high = value.astype(jnp.bfloat16)
    low = (value - high.astype(jnp.float32)).astype(jnp.bfloat16)
    return high, low


def product(first, second, dims=NN):
    dot = functools.partial(
        lax.dot_general, dimension_numbers=dims, preferred_element_type=jnp.float32
    )
    return dot(first[0], second[0]) + (dot(first[0], second[1]) + dot(first[1], second[0]))


def flipped(index, mask):
    bit = 1
    while bit <= mask:
        if mask & bit:
            index = index + bit * (1 - 2 * (lax.div(index, bit) % 2))
        bit *= 2
    return index


def kernel(
    n_mem, n_reg, block_ref, ens_ref, obs_ref, innov_ref, weight_ref, out_ref,
    obs_all, innov_all, columns, result, gram, drive_parts,
    local_sem, obs_send, obs_recv, halo_send, halo_recv, innov_send, innov_recv,
    ens_send, ens_recv, out_send, out_recv,
):
    me, region = lax.axis_index("mem"), lax.axis_index("reg")
    rows = obs_ref.shape[0]
    members = n_mem * rows
    own_obs = obs_ref.shape[1]
    points = columns.shape[1]
    listed, width = weight_ref.shape
    own_blocks = own_obs // width
    has_before, has_after = region > 0, region < n_reg - 1
    sides = ((has_before, region - 1, 0), (has_after, region + 1, 1))

    def rows_of(which):
        return pl.ds(pl.multiple_of(which * rows, rows), rows)

    parts_in = obs_send.shape[1]
    part = rows // parts_in

    def part_of(which, at):
        return pl.ds(pl.multiple_of(which * rows + at * part, part), part)

    def points_of(which):
        return pl.ds(pl.multiple_of(which * points, points), points)

    barrier = pltpu.get_barrier_semaphore()
    for step in range(1, n_mem):
        pl.semaphore_signal(
            barrier, inc=1, device_id=(flipped(me, step), region), device_id_type=MESH
        )
    for there, other, side in sides:
        @pl.when(there)
        def _():
            pl.semaphore_signal(barrier, inc=1, device_id=(me, other), device_id_type=MESH)

    own_obs_copy = pltpu.make_async_copy(obs_ref, obs_all.at[1, rows_of(me)], local_sem.at[0])
    own_obs_copy.start()
    own_innov_copy = pltpu.make_async_copy(innov_ref, innov_all.at[1], local_sem.at[1])
    own_innov_copy.start()
    own_ens_copy = pltpu.make_async_copy(
        ens_ref.at[:, points_of(me)], columns.at[rows_of(me)], local_sem.at[2]
    )
    own_ens_copy.start()

    near = has_before.astype(jnp.int32) + has_after.astype(jnp.int32)
    pl.semaphore_wait(barrier, n_mem - 1 + near)

    relay = n_mem == 4 and parts_in > 1
    direct = n_mem - 1 if relay else n_mem

    def gather(step, at):
        if relay and step == 3:
            source, target = (2, 1) if at % 2 == 0 else (1, 2)
            piece = part_of(flipped(me, source), at)
            return pltpu.make_async_remote_copy(
                src_ref=obs_all.at[1, piece], dst_ref=obs_all.at[1, piece],
                send_sem=obs_send.at[step, at], recv_sem=obs_recv.at[step, at],
                device_id=(flipped(me, target), region), device_id_type=MESH,
            )
        return pltpu.make_async_remote_copy(
            src_ref=obs_ref.at[pl.ds(at * part, part)], dst_ref=obs_all.at[1, part_of(me, at)],
            send_sem=obs_send.at[step, at], recv_sem=obs_recv.at[step, at],
            device_id=(flipped(me, step), region), device_id_type=MESH,
        )

    def halo(step, at, other, side):
        piece = part_of(flipped(me, step), at)
        return pltpu.make_async_remote_copy(
            src_ref=obs_ref.at[pl.ds(at * part, part)] if step == 0 else obs_all.at[1, piece],
            dst_ref=obs_all.at[2 - 2 * side, piece],
            send_sem=halo_send.at[side, step, at], recv_sem=halo_recv.at[side, step, at],
            device_id=(me, other), device_id_type=MESH,
        )

    def innov(other, side):
        return pltpu.make_async_remote_copy(
            src_ref=innov_ref, dst_ref=innov_all.at[2 - 2 * side],
            send_sem=innov_send.at[side], recv_sem=innov_recv.at[side],
            device_id=(me, other), device_id_type=MESH,
        )

    def exchange(step):
        other = flipped(me, step)
        return pltpu.make_async_remote_copy(
            src_ref=ens_ref.at[:, points_of(other)], dst_ref=columns.at[rows_of(me)],
            send_sem=ens_send.at[step], recv_sem=ens_recv.at[step],
            device_id=(other, region), device_id_type=MESH,
        )

    def give_back(step):
        other = flipped(me, step)
        return pltpu.make_async_remote_copy(
            src_ref=result.at[rows_of(other)], dst_ref=out_ref.at[:, points_of(me)],
            send_sem=out_send.at[step], recv_sem=out_recv.at[step],
            device_id=(other, region), device_id_type=MESH,
        )

    for at in range(parts_in):
        for step in range(1, direct):
            gather(step, at).start()
    for there, other, side in sides:
        @pl.when(there)
        def _():
            for at in range(parts_in):
                halo(0, at, other, side).start()
            innov(other, side).start()
    for step in range(1, n_mem):
        exchange(step).start()
    def pass_on(step, at):
        gather(step, at).wait_recv()
        if relay and (step == 1 and at % 2 == 1 or step == 2 and at % 2 == 0):
            gather(3, at).start()
        for there, other, side in sides:
            @pl.when(there)
            def _():
                halo(step, at, other, side).start()

    for at in range(parts_in):
        for step in range(1, direct):
            pass_on(step, at)
    for at in range(parts_in):
        for step in range(direct, n_mem):
            pass_on(step, at)

    own_ens_copy.wait()
    for step in range(1, n_mem):
        exchange(step).wait_recv()
    ensemble = columns[...]
    mean = jnp.sum(ensemble, axis=0, keepdims=True) / members
    anomalies = ensemble - mean
    anomaly_halves = halves(anomalies)

    def add_region(slot):
        first = (region - 1 + slot) * own_blocks
        parts = []
        for at in range(own_blocks):
            chosen = jnp.where(block_ref[...] == first + at, weight_ref[...], 0.0)
            parts.append(jnp.sum(chosen, axis=0, keepdims=True))
        block = obs_all[slot]
        scaled = block * jnp.concatenate(parts, axis=1)
        gram[...] += product(halves(scaled), halves(block), NT)
        driven = scaled * innov_all[slot]
        total = driven[:, :width]
        for at in range(1, own_blocks):
            total = total + driven[:, at * width : (at + 1) * width]
        drive_parts[...] += total

    gram[...] = jnp.zeros_like(gram)
    drive_parts[...] = jnp.zeros_like(drive_parts)
    own_obs_copy.wait()
    own_innov_copy.wait()
    add_region(1)
    for there, other, side in sides:
        @pl.when(there)
        def _():
            for step in range(n_mem):
                for at in range(parts_in):
                    halo(step, at, other, 1 - side).wait_recv()
            innov(other, 1 - side).wait_recv()
            add_region(2 * side)

    row_at = lax.broadcasted_iota(jnp.int32, (members, members), 0)
    column_at = lax.broadcasted_iota(jnp.int32, (members, members), 1)
    diagonal = row_at == column_at
    identity = jnp.where(diagonal, 1.0, 0.0)
    drive = jnp.sum(drive_parts[...], axis=1, keepdims=True)

    system = identity + gram[...] / (members - 1.0)
    trace = jnp.sum(jnp.where(diagonal, system, 0.0), axis=0, keepdims=True)
    trace = jnp.sum(trace, axis=1, keepdims=True)
    iterate_y = system / trace
    factor = 1.5 * identity - 0.5 * iterate_y
    factor_halves = halves(factor)
    iterate_y = product(halves(iterate_y), factor_halves)
    iterate_z = factor
    z_halves = factor_halves
    for repeat in range(1, NEWTON):
        y_halves = halves(iterate_y)
        factor_halves = halves(1.5 * identity - 0.5 * product(z_halves, y_halves))
        if repeat < NEWTON - 1:
            iterate_y = product(y_halves, factor_halves)
        iterate_z = product(factor_halves, z_halves)
        z_halves = halves(iterate_z)
    root = iterate_z * lax.rsqrt(trace)
    half_step = jnp.sum(root * drive, axis=0, keepdims=True)
    mean_weights = jnp.sum(root * half_step, axis=1, keepdims=True) / (members - 1.0)
    shift = mean + jnp.sum(anomalies * mean_weights, axis=0, keepdims=True)
    result[...] = shift + product(halves(root), anomaly_halves)

    for step in range(1, n_mem):
        give_back(step).start()
    own_out = pltpu.make_async_copy(
        result.at[rows_of(me)], out_ref.at[:, points_of(me)], local_sem.at[3]
    )
    own_out.start()
    for step in range(1, n_mem):
        for at in range(parts_in):
            gather(step, at).wait_send()
        exchange(step).wait_send()
    for there, other, side in sides:
        @pl.when(there)
        def _():
            for step in range(n_mem):
                for at in range(parts_in):
                    halo(step, at, other, side).wait_send()
            innov(other, side).wait_send()
    own_out.wait()
    for step in range(1, n_mem):
        give_back(step).wait()


def on_device(ensemble, obs_pert, innovation, block_list, loc_weights):
    n_mem, n_reg = lax.axis_size("mem"), lax.axis_size("reg")
    rows, own_points = ensemble.shape
    own_obs = obs_pert.shape[1]
    listed, width = loc_weights.shape[1:]
    members, points = rows * n_mem, own_points // n_mem
    parts_in = 4 if rows % 32 == 0 else 2 if rows % 16 == 0 else 1
    return pl.pallas_call(
        functools.partial(kernel, n_mem, n_reg),
        out_shape=jax.ShapeDtypeStruct((rows, own_points), jnp.float32),
        in_specs=[
            pl.BlockSpec(memory_space=pltpu.VMEM),
            pl.BlockSpec(memory_space=pl.ANY),
            pl.BlockSpec(memory_space=pl.ANY),
            pl.BlockSpec(memory_space=pltpu.VMEM),
            pl.BlockSpec(memory_space=pltpu.VMEM),
        ],
        out_specs=pl.BlockSpec(memory_space=pl.ANY),
        scratch_shapes=[
            pltpu.VMEM((3, members, own_obs), jnp.float32),
            pltpu.VMEM((3, 1, own_obs), jnp.float32),
            pltpu.VMEM((members, points), jnp.float32),
            pltpu.VMEM((members, points), jnp.float32),
            pltpu.VMEM((members, members), jnp.float32),
            pltpu.VMEM((members, width), jnp.float32),
            pltpu.SemaphoreType.DMA((4,)),
            pltpu.SemaphoreType.DMA((n_mem, parts_in)),
            pltpu.SemaphoreType.DMA((n_mem, parts_in)),
            pltpu.SemaphoreType.DMA((2, n_mem, parts_in)),
            pltpu.SemaphoreType.DMA((2, n_mem, parts_in)),
            pltpu.SemaphoreType.DMA((2,)),
            pltpu.SemaphoreType.DMA((2,)),
            pltpu.SemaphoreType.DMA((n_mem,)),
            pltpu.SemaphoreType.DMA((n_mem,)),
            pltpu.SemaphoreType.DMA((n_mem,)),
            pltpu.SemaphoreType.DMA((n_mem,)),
        ],
        compiler_params=pltpu.CompilerParams(
            collective_id=0, has_side_effects=True, vmem_limit_bytes=32 * 2**20
        ),
    )(
        block_list.reshape(listed, 1), ensemble, obs_pert,
        innovation.reshape(1, own_obs), loc_weights.reshape(listed, width),
    )


def solution(mesh):
    return jax.shard_map(
        on_device,
        mesh=mesh,
        in_specs=(
            P("mem", "reg"),
            P("mem", "reg"),
            P("reg"),
            P(("reg", "mem"), None),
            P(("reg", "mem"), None, None),
        ),
        out_specs=P("mem", "reg"),
        check_vma=False,
    )
```

```python
import functools

import jax
import jax.numpy as jnp
from jax import lax
from jax.experimental import pallas as pl
from jax.experimental.pallas import tpu as pltpu
from jax.sharding import PartitionSpec as P

NEWTON = 8
MESH = pl.DeviceIdType.MESH
NN = (((1,), (0,)), ((), ()))
NT = (((1,), (1,)), ((), ()))


def halves(value):
    high = value.astype(jnp.bfloat16)
    low = (value - high.astype(jnp.float32)).astype(jnp.bfloat16)
    return high, low


def product(first, second, dims=NN):
    dot = functools.partial(
        lax.dot_general, dimension_numbers=dims, preferred_element_type=jnp.float32
    )
    return dot(first[0], second[0]) + (dot(first[0], second[1]) + dot(first[1], second[0]))


def flipped(index, mask):
    bit = 1
    while bit <= mask:
        if mask & bit:
            index = index + bit * (1 - 2 * (lax.div(index, bit) % 2))
        bit *= 2
    return index


def kernel(
    n_mem, n_reg, block_ref, ens_ref, obs_ref, innov_ref, weight_ref, out_ref,
    obs_all, innov_all, columns, result, gram, drive_parts,
    local_sem, obs_send, obs_recv, halo_send, halo_recv, innov_send, innov_recv,
    ens_send, ens_recv, out_send, out_recv,
):
    me, region = lax.axis_index("mem"), lax.axis_index("reg")
    rows = obs_ref.shape[0]
    members = n_mem * rows
    own_obs = obs_ref.shape[1]
    points = columns.shape[1]
    listed, width = weight_ref.shape
    own_blocks = own_obs // width
    has_before, has_after = region > 0, region < n_reg - 1
    sides = ((has_before, region - 1, 0), (has_after, region + 1, 1))

    def rows_of(which):
        return pl.ds(pl.multiple_of(which * rows, rows), rows)

    parts_in = obs_send.shape[1]
    part = own_obs // parts_in
    part_blocks = part // width

    def part_of(slot, which, at):
        return obs_all.at[slot, rows_of(which), pl.ds(at * part, part)]

    def points_of(which):
        return pl.ds(pl.multiple_of(which * points, points), points)

    barrier = pltpu.get_barrier_semaphore()
    for step in range(1, n_mem):
        pl.semaphore_signal(
            barrier, inc=1, device_id=(flipped(me, step), region), device_id_type=MESH
        )
    for there, other, side in sides:
        @pl.when(there)
        def _():
            pl.semaphore_signal(barrier, inc=1, device_id=(me, other), device_id_type=MESH)

    own_obs_copy = pltpu.make_async_copy(obs_ref, obs_all.at[1, rows_of(me)], local_sem.at[0])
    own_obs_copy.start()
    own_innov_copy = pltpu.make_async_copy(innov_ref, innov_all.at[1], local_sem.at[1])
    own_innov_copy.start()
    own_ens_copy = pltpu.make_async_copy(
        ens_ref.at[:, points_of(me)], columns.at[rows_of(me)], local_sem.at[2]
    )
    own_ens_copy.start()

    near = has_before.astype(jnp.int32) + has_after.astype(jnp.int32)
    pl.semaphore_wait(barrier, n_mem - 1 + near)

    relay = n_mem == 4 and parts_in > 1
    direct = n_mem - 1 if relay else n_mem

    def gather(step, at):
        if relay and step == 3:
            source, target = (2, 1) if at % 2 == 0 else (1, 2)
            piece = part_of(1, flipped(me, source), at)
            return pltpu.make_async_remote_copy(
                src_ref=piece, dst_ref=piece,
                send_sem=obs_send.at[step, at], recv_sem=obs_recv.at[step, at],
                device_id=(flipped(me, target), region), device_id_type=MESH,
            )
        return pltpu.make_async_remote_copy(
            src_ref=obs_ref.at[:, pl.ds(at * part, part)], dst_ref=part_of(1, me, at),
            send_sem=obs_send.at[step, at], recv_sem=obs_recv.at[step, at],
            device_id=(flipped(me, step), region), device_id_type=MESH,
        )

    def halo(step, at, other, side):
        owner = flipped(me, step)
        return pltpu.make_async_remote_copy(
            src_ref=obs_ref.at[:, pl.ds(at * part, part)] if step == 0 else part_of(1, owner, at),
            dst_ref=part_of(2 - 2 * side, owner, at),
            send_sem=halo_send.at[side, step, at], recv_sem=halo_recv.at[side, step, at],
            device_id=(me, other), device_id_type=MESH,
        )

    def innov(other, side):
        return pltpu.make_async_remote_copy(
            src_ref=innov_ref, dst_ref=innov_all.at[2 - 2 * side],
            send_sem=innov_send.at[side], recv_sem=innov_recv.at[side],
            device_id=(me, other), device_id_type=MESH,
        )

    def exchange(step):
        other = flipped(me, step)
        return pltpu.make_async_remote_copy(
            src_ref=ens_ref.at[:, points_of(other)], dst_ref=columns.at[rows_of(me)],
            send_sem=ens_send.at[step], recv_sem=ens_recv.at[step],
            device_id=(other, region), device_id_type=MESH,
        )

    def give_back(step):
        other = flipped(me, step)
        return pltpu.make_async_remote_copy(
            src_ref=result.at[rows_of(other)], dst_ref=out_ref.at[:, points_of(me)],
            send_sem=out_send.at[step], recv_sem=out_recv.at[step],
            device_id=(other, region), device_id_type=MESH,
        )

    for at in range(parts_in):
        for step in range(1, direct):
            gather(step, at).start()
    for there, other, side in sides:
        @pl.when(there)
        def _():
            for at in range(parts_in):
                halo(0, at, other, side).start()
            innov(other, side).start()
    for step in range(1, n_mem):
        exchange(step).start()
    def pass_on(step, at):
        gather(step, at).wait_recv()
        if relay and (step == 1 and at % 2 == 1 or step == 2 and at % 2 == 0):
            gather(3, at).start()
        for there, other, side in sides:
            @pl.when(there)
            def _():
                halo(step, at, other, side).start()

    for at in range(parts_in):
        for step in range(1, direct):
            pass_on(step, at)
        for step in range(direct, n_mem):
            if at > 0:
                pass_on(step, at - 1)
    for step in range(direct, n_mem):
        pass_on(step, parts_in - 1)

    own_ens_copy.wait()
    for step in range(1, n_mem):
        exchange(step).wait_recv()
    ensemble = columns[...]
    mean = jnp.sum(ensemble, axis=0, keepdims=True) / members
    anomalies = ensemble - mean
    anomaly_halves = halves(anomalies)

    def add_part(slot, piece):
        first = (region - 1 + slot) * own_blocks + piece * part_blocks
        parts = []
        for at in range(part_blocks):
            chosen = jnp.where(block_ref[...] == first + at, weight_ref[...], 0.0)
            parts.append(jnp.sum(chosen, axis=0, keepdims=True))
        columns_here = slice(piece * part, (piece + 1) * part)
        block = obs_all[slot, :, columns_here]
        scaled = block * jnp.concatenate(parts, axis=1)
        gram[...] += product(halves(scaled), halves(block), NT)
        driven = scaled * innov_all[slot, :, columns_here]
        total = driven[:, :width]
        for at in range(1, part_blocks):
            total = total + driven[:, at * width : (at + 1) * width]
        drive_parts[...] += total

    gram[...] = jnp.zeros_like(gram)
    drive_parts[...] = jnp.zeros_like(drive_parts)
    own_obs_copy.wait()
    own_innov_copy.wait()
    for at in range(parts_in):
        add_part(1, at)
    for there, other, side in sides:
        @pl.when(there)
        def _():
            innov(other, 1 - side).wait_recv()
    for at in range(parts_in):
        for there, other, side in sides:
            @pl.when(there)
            def _():
                for step in range(n_mem):
                    halo(step, at, other, 1 - side).wait_recv()
                add_part(2 * side, at)

    row_at = lax.broadcasted_iota(jnp.int32, (members, members), 0)
    column_at = lax.broadcasted_iota(jnp.int32, (members, members), 1)
    diagonal = row_at == column_at
    identity = jnp.where(diagonal, 1.0, 0.0)
    drive = jnp.sum(drive_parts[...], axis=1, keepdims=True)

    system = identity + gram[...] / (members - 1.0)
    trace = jnp.sum(jnp.where(diagonal, system, 0.0), axis=0, keepdims=True)
    trace = jnp.sum(trace, axis=1, keepdims=True)
    iterate_y = system / trace
    factor = 1.5 * identity - 0.5 * iterate_y
    factor_halves = halves(factor)
    iterate_y = product(halves(iterate_y), factor_halves)
    iterate_z = factor
    z_halves = factor_halves
    for repeat in range(1, NEWTON):
        y_halves = halves(iterate_y)
        factor_halves = halves(1.5 * identity - 0.5 * product(z_halves, y_halves))
        if repeat < NEWTON - 1:
            iterate_y = product(y_halves, factor_halves)
        iterate_z = product(factor_halves, z_halves)
        z_halves = halves(iterate_z)
    root = iterate_z * lax.rsqrt(trace)
    half_step = jnp.sum(root * drive, axis=0, keepdims=True)
    mean_weights = jnp.sum(root * half_step, axis=1, keepdims=True) / (members - 1.0)
    shift = mean + jnp.sum(anomalies * mean_weights, axis=0, keepdims=True)
    result[...] = shift + product(halves(root), anomaly_halves)

    for step in range(1, n_mem):
        give_back(step).start()
    own_out = pltpu.make_async_copy(
        result.at[rows_of(me)], out_ref.at[:, points_of(me)], local_sem.at[3]
    )
    own_out.start()
    for step in range(1, n_mem):
        for at in range(parts_in):
            gather(step, at).wait_send()
        exchange(step).wait_send()
    for there, other, side in sides:
        @pl.when(there)
        def _():
            for step in range(n_mem):
                for at in range(parts_in):
                    halo(step, at, other, side).wait_send()
            innov(other, side).wait_send()
    own_out.wait()
    for step in range(1, n_mem):
        give_back(step).wait()


def on_device(ensemble, obs_pert, innovation, block_list, loc_weights):
    n_mem, n_reg = lax.axis_size("mem"), lax.axis_size("reg")
    rows, own_points = ensemble.shape
    own_obs = obs_pert.shape[1]
    listed, width = loc_weights.shape[1:]
    members, points = rows * n_mem, own_points // n_mem
    blocks = own_obs // width
    parts_in = 4 if blocks % 4 == 0 else 2 if blocks % 2 == 0 else 1
    return pl.pallas_call(
        functools.partial(kernel, n_mem, n_reg),
        out_shape=jax.ShapeDtypeStruct((rows, own_points), jnp.float32),
        in_specs=[
            pl.BlockSpec(memory_space=pltpu.VMEM),
            pl.BlockSpec(memory_space=pl.ANY),
            pl.BlockSpec(memory_space=pl.ANY),
            pl.BlockSpec(memory_space=pltpu.VMEM),
            pl.BlockSpec(memory_space=pltpu.VMEM),
        ],
        out_specs=pl.BlockSpec(memory_space=pl.ANY),
        scratch_shapes=[
            pltpu.VMEM((3, members, own_obs), jnp.float32),
            pltpu.VMEM((3, 1, own_obs), jnp.float32),
            pltpu.VMEM((members, points), jnp.float32),
            pltpu.VMEM((members, points), jnp.float32),
            pltpu.VMEM((members, members), jnp.float32),
            pltpu.VMEM((members, width), jnp.float32),
            pltpu.SemaphoreType.DMA((4,)),
            pltpu.SemaphoreType.DMA((n_mem, parts_in)),
            pltpu.SemaphoreType.DMA((n_mem, parts_in)),
            pltpu.SemaphoreType.DMA((2, n_mem, parts_in)),
            pltpu.SemaphoreType.DMA((2, n_mem, parts_in)),
            pltpu.SemaphoreType.DMA((2,)),
            pltpu.SemaphoreType.DMA((2,)),
            pltpu.SemaphoreType.DMA((n_mem,)),
            pltpu.SemaphoreType.DMA((n_mem,)),
            pltpu.SemaphoreType.DMA((n_mem,)),
            pltpu.SemaphoreType.DMA((n_mem,)),
        ],
        compiler_params=pltpu.CompilerParams(
            collective_id=0, has_side_effects=True, vmem_limit_bytes=32 * 2**20
        ),
    )(
        block_list.reshape(listed, 1), ensemble, obs_pert,
        innovation.reshape(1, own_obs), loc_weights.reshape(listed, width),
    )


def solution(mesh):
    return jax.shard_map(
        on_device,
        mesh=mesh,
        in_specs=(
            P("mem", "reg"),
            P("mem", "reg"),
            P("reg"),
            P(("reg", "mem"), None),
            P(("reg", "mem"), None, None),
        ),
        out_specs=P("mem", "reg"),
        check_vma=False,
    )
```
